768 devices in a mesh: section: 6 (over z_hi, core), expert: 4 (over x), dp: 32 (over z_lo, y).
Axes of the slice: x: 4, y: 8, z: 12 (z_hi: 3, z_lo: 4; z = z_hi * 4 + z_lo), core: 2. Of those that a mesh axis runs over, the one named last changes fastest.
Arguments:
- grad_out: bfloat16 [6, 512, 4096], P('section', 'expert', 'dp'), may hold values from -6 to 6
- routes: int32 [6, 512, 2], P('section', 'expert'), may hold values from 0 to 3, all different within a row; in each aligned block of 128 rows (0 to 127, 128 to 255, ..., all dimensions but the last counted through in order) at most 128 rows name the same one
- route_prob: float32 [6, 512, 2], P('section', 'expert'), may hold values from 0.05 to 1
- saved_gate: bfloat16 [6, 4, 512, 768], P('section', 'expert'), may hold values from -6 to 6
- saved_up: bfloat16 [6, 4, 512, 768], P('section', 'expert'), may hold values from -6 to 6
- w_gate: bfloat16 [6, 4, 4096, 768], P('section', 'expert', 'dp'), may hold values from -0.09375 to 0.09375
- w_up: bfloat16 [6, 4, 4096, 768], P('section', 'expert', 'dp'), may hold values from -0.09375 to 0.09375
- w_down: bfloat16 [6, 4, 768, 4096], P('section', 'expert', None, 'dp'), may hold values from -0.21875 to 0.21875
Outputs:
- upstream: bfloat16 [6, 512, 4096], P('section', 'expert', 'dp')
- grad_down: bfloat16 [6, 4, 768, 4096], P('section', 'expert', None, 'dp')
The draws below stay inside these ranges and needn't reach their ends.
Inputs may be any that keep to these rules, and one draw needn't show every extreme that they name: Each token's 2 ids are distinct; within each aligned block of 128 tokens no expert is named by more than 128 routes, and in every draw some expert is named by exactly 128 routes of some block.
All inputs are finite; a program needn't handle non-finite values.
Results may differ from the reference program's by a relative error of at most 0.0057.
Values may be sent and summed in bfloat16 or wider, within the bound.
A program may use at most 32 MiB of HBM per device.

```python
import math
import jax
import jax.numpy as jnp
import numpy as np
from jax import lax

D = 4096
HID = 768
TOP = 2
TOK = 128
EXPERTS = 4
CAP = 128
SLOTS = 512
TOKENS = 512
N_SECTION = 6
N_EXPERT = 4


def steps_of(stream_key, shape, cuts, smallest, high):
    level = 1.0
    for dim, shards_of in cuts:
        draws = jax.random.uniform(jax.random.fold_in(jax.random.fold_in(stream_key, 6), dim), (shards_of,), jnp.float32, smallest / len(cuts), high / len(cuts))
        level = level * jnp.repeat(jnp.exp(draws), shape[dim] // shards_of).reshape((-1,) + (1,) * (len(shape) - 1 - dim))
    return level


def routed_block(rng, own, number, rows, amount, top, reach, slope):
    ranking = jax.random.permutation(rng, amount)
    crowded, ordinary = shares(amount, rows * top, reach, slope, True), shares(amount, rows * top, reach, slope, False)
    places = jnp.arange(amount)

    def named(lengths, offset_by):
        used = int((lengths > 0).sum())
        fixed = max(1, used // 4)
        moved = fixed + (places - fixed + offset_by * (used - fixed)) % max(1, amount - fixed)
        return jnp.zeros((amount,), jnp.int32).at[ranking[jnp.where(places < fixed, places, moved)]].set(jnp.asarray(lengths, jnp.int32))

    lengths = jnp.where(number % 4 == 0, named(crowded, number // 4), named(ordinary, number - number // 4 - 1))
    mixed = jax.random.permutation(jax.random.fold_in(own, 3), amount)
    donor, receiver = mixed[0:amount // 2 * 2:2], mixed[1:amount // 2 * 2:2]
    margin = jnp.minimum(lengths[donor] - 1, reach - lengths[receiver]) // 2
    margin = jnp.where((donor == ranking[0]) | (receiver == ranking[0]) | (lengths[receiver] == 0), 0, jnp.maximum(margin, 0))
    moved = jax.random.randint(jax.random.fold_in(own, 4), (amount // 2,), 0, 1 << 20) % (margin + 1)
    lengths = lengths.at[donor].add(-moved).at[receiver].add(moved)
    items = jnp.searchsorted(jnp.cumsum(lengths), jnp.arange(rows * top), side="right").astype(jnp.int32)
    table = items.reshape(top, rows).T
    table = table[jax.random.permutation(jax.random.fold_in(own, 1), rows)]
    offset_by = jax.random.randint(jax.random.fold_in(own, 2), (rows, 1), 0, top)
    return jnp.take_along_axis(table, (jnp.arange(top)[None, :] + offset_by) % top, axis=1)


def shares(count, total, reach, slope, full):
    portions = [(1 << 20) // math.isqrt(grade ** slope) + 1 for grade in range(1, count + 1)]
    largest = reach if full else min(reach, max(-(-total // count), total * portions[0] // sum(portions)))
    least = 1 if total - largest >= count - 1 else 0
    holding, rest = [largest] + [least] * (count - 1), total - largest - least * (count - 1)
    while rest > 0:
        movable = [i for i in range(1, count) if holding[i] < largest] or [i for i in range(1, count) if holding[i] < reach]
        pool, remaining = sum([portions[i] for i in movable]), rest
        for i in movable:
            addition = min(reach - holding[i], max(1, remaining * portions[i] // pool), rest)
            holding[i] = holding[i] + addition
            rest = rest - addition
    return np.array(holding)


def scatter_about(key, dims, spread, most, split=(), kind=jnp.bfloat16):
    result = jax.random.normal(key, dims, jnp.float32) * spread
    if len(split) > 0:
        result = steps_of(key, dims, split, -0.22, 0.18) * result
    return jnp.clip(result, min=-most, max=most).astype(kind)


def setup_inputs(seed: int = 0) -> dict:
    streams_of = jax.random.split(jax.random.key(seed), 9)
    grad_out = scatter_about(streams_of[0], (N_SECTION, TOKENS, D), 1.0, 6.0, ((0, 6), (1, 4), (2, 32)))
    routes_keys = jax.random.split(jax.random.fold_in(streams_of[1], 1), N_SECTION * TOKENS // TOK)
    routes_turns = jax.random.permutation(jax.random.fold_in(streams_of[1], 3), N_SECTION * TOKENS // TOK)
    routes = jax.vmap(lambda own, number: routed_block(jax.random.fold_in(streams_of[1], 2), own, number, TOK, EXPERTS, TOP, CAP, 2))(routes_keys, routes_turns).reshape((N_SECTION, TOKENS, TOP))
    route_prob = jnp.clip(jnp.exp(math.log(1.0) - 2.9957323 * jax.random.uniform(streams_of[2], (N_SECTION, TOKENS, TOP), jnp.float32) ** steps_of(streams_of[2], (N_SECTION, TOKENS, TOP), ((0, 6), (1, 4)), -0.2, 0.2)), 0.05, 1.0)
    saved_gate = scatter_about(streams_of[3], (N_SECTION, EXPERTS, SLOTS, HID), 1.0, 6.0, ((0, 6), (1, 4)))
    saved_up = scatter_about(streams_of[4], (N_SECTION, EXPERTS, SLOTS, HID), 1.0, 6.0, ((0, 6), (1, 4)))
    w_gate = scatter_about(streams_of[5], (N_SECTION, EXPERTS, D, HID), D ** -0.5, 0.09375, ((0, 6), (1, 4), (2, 32)))
    w_up = scatter_about(streams_of[6], (N_SECTION, EXPERTS, D, HID), D ** -0.5, 0.09375, ((0, 6), (1, 4), (2, 32)))
    w_down = scatter_about(streams_of[7], (N_SECTION, EXPERTS, HID, D), HID ** -0.5, 0.21875, ((0, 6), (1, 4), (3, 32)))
    return {"grad_out": grad_out, "routes": routes, "route_prob": route_prob, "saved_gate": saved_gate, "saved_up": saved_up, "w_gate": w_gate, "w_up": w_up, "w_down": w_down}


def expert_pass(pieces):
    received, gate_raw, up_raw, gate_weight, up_weight, down_weight = pieces
    act_grad = jnp.dot(received, down_weight.T, preferred_element_type=jnp.float32)
    gate_in = gate_raw.astype(jnp.float32)
    up_in = up_raw.astype(jnp.float32)
    sigmoid_gate = jax.nn.sigmoid(gate_in)
    swished = gate_in * sigmoid_gate
    gate_grad = (act_grad * up_in * sigmoid_gate * (1.0 + gate_in * (1.0 - sigmoid_gate))).astype(jnp.bfloat16)
    up_grad = (act_grad * swished).astype(jnp.bfloat16)
    slot_grads = jnp.dot(gate_grad, gate_weight.T, preferred_element_type=jnp.float32)
    slot_grads = (slot_grads + jnp.dot(up_grad, up_weight.T, preferred_element_type=jnp.float32)).astype(jnp.bfloat16)
    activated = (swished * up_in).astype(jnp.bfloat16)
    down_grad = jnp.dot(activated.T, received, preferred_element_type=jnp.float32).astype(jnp.bfloat16)
    return slot_grads, down_grad


def segment_pass(pieces):
    gradient, expert_ids, weights, gate_all, up_all, gate_w, up_w, down_w = pieces
    group_ids = expert_ids.reshape(N_EXPERT, TOK * TOP)
    matches = (group_ids[:, :, None] == jnp.arange(EXPERTS, dtype=jnp.int32)[None, None, :]).astype(jnp.int32)
    ordinal = jnp.sum((jnp.cumsum(matches, axis=1) - 1) * matches, axis=2)
    source = jnp.arange(N_EXPERT, dtype=jnp.int32)[:, None] * CAP
    position = (source + ordinal).reshape(-1).astype(jnp.int32)
    target = group_ids.reshape(-1).astype(jnp.int32)
    routed = (weights[:, :, None] * gradient[:, None, :].astype(jnp.float32)).astype(jnp.bfloat16)
    routed = routed.reshape(TOKENS * TOP, D)
    buffer = jnp.zeros((EXPERTS, SLOTS, D), jnp.bfloat16).at[target, position].set(routed)
    slot_grads, down_grad = lax.map(expert_pass, (buffer, gate_all, up_all, gate_w, up_w, down_w))
    picked = slot_grads[target, position].astype(jnp.float32).reshape(TOKENS, TOP, D)
    input_grad = (gradient.astype(jnp.float32) + jnp.sum(picked, axis=1)).astype(jnp.bfloat16)
    return input_grad, down_grad


def reference(grad_out, routes, route_prob, saved_gate, saved_up, w_gate, w_up, w_down):
    input_grad, grad_down = lax.map(segment_pass, (grad_out, routes, route_prob, saved_gate, saved_up, w_gate, w_up, w_down))
    upstream = jnp.concatenate([input_grad[1:], jnp.zeros_like(input_grad[:1])], axis=0)
    return upstream, grad_down
```

```python
import functools

import jax
import jax.numpy as jnp
from jax import lax
from jax.experimental import pallas as pl
from jax.experimental.pallas import tpu as pltpu
from jax.sharding import PartitionSpec as P

MESH = pl.DeviceIdType.MESH
F32 = jnp.float32
BF16 = jnp.bfloat16

NX, NY, NZ, NS = 4, 8, 4, 6
TOK, FEAT, HID = 128, 128, 768
CA = 384
CB = HID - CA
RY, RZ = TOK // NY, TOK // NZ
Y_ORDER = (4, 3, 5, 2, 6, 1, 7)
Z_ORDER = (2, 1, 3)


def spans(start, stop, step):
    return [(at, min(step, stop - at)) for at in range(start, stop, step)]


def dot_nt(left, right):
    return lax.dot_general(left, right, (((1,), (1,)), ((), ())), preferred_element_type=F32)


def dot_tn(left, right):
    return lax.dot_general(left, right, (((0,), (0,)), ((), ())), preferred_element_type=F32)


def kernel(
    grad_h, routes_h, prob_h, sg_h, su_h, wg_h, wu_h, wd_h,
    up_out, gd_out,
    grads, meta, routes, prob, sg, su, wg, wu, wd,
    pa, pb, ra, rb, sa, sb, r2a, r2b, acta, actb,
    fgate, fup, activated, routed, mine, ret, ubuf, vbuf,
    load_sem, x_send, x_recv, m_recv, s1a_send, s1a_recv, s1b_send, s1b_recv,
    s2a_send, s2a_recv, s2b_send, s2b_recv,
    g1a_send, g1a_recv, g1b_send, g1b_recv, g2a_send, g2a_recv, g2b_send, g2b_recv,
    ret_send, ret_recv, sec_send, sec_recv,
):
    s = lax.axis_index("section")
    x = lax.axis_index("expert")
    d = lax.axis_index("dp")
    y = d % NY
    z = d // NY

    def at_y(k):
        return (y + k) % NY

    def at_z(k):
        return (z + k) % NZ

    def dp(zz, yy):
        return {"dp": zz * NY + yy}

    def copy(src, dst, send, recv, device):
        return pltpu.make_async_remote_copy(
            src_ref=src, dst_ref=dst, send_sem=send, recv_sem=recv,
            device_id=device, device_id_type=MESH,
        )

    def await_recv(ref, sem):
        copy(ref, ref, sem, sem, dp(z, y)).wait_recv()

    def await_send(ref, sem):
        copy(ref, ref, sem, sem, dp(z, y)).wait_send()

    loads = {}
    for number, (name, src, dst) in enumerate((
        ("grad", grad_h, grads.at[0]), ("routes", routes_h, routes), ("prob", prob_h, prob),
        ("wd", wd_h, wd), ("sg", sg_h, sg), ("su", su_h, su), ("wg", wg_h, wg), ("wu", wu_h, wu),
    )):
        loads[name] = pltpu.make_async_copy(src, dst, load_sem.at[number])
        loads[name].start()

    barrier = pltpu.get_barrier_semaphore()
    greet = [dp(z, at_y(k)) for k in range(1, NY)] + [dp(at_z(k), y) for k in range(1, NZ)]
    greet += [{"expert": (x + k) % NX} for k in range(1, NX)]
    greet += [{"section": (s + 1) % NS}]
    for device in greet:
        pl.semaphore_signal(barrier, inc=1, device_id=device, device_id_type=MESH)

    for name in ("grad", "routes", "prob"):
        loads[name].wait()
    meta[0, 0:2, :] = prob[...]
    meta[0, 2:4, :] = routes[...].astype(F32)
    meta[0, 4:8, :] = jnp.zeros((4, TOK), F32)

    def make_partial(j):
        for at, size in spans(0, CA, 256):
            pa[j, :, at:at + size] = dot_nt(grads[j], wd[at:at + size, :]).astype(BF16)
        for at, size in spans(0, CB, 256):
            pb[j, :, at:at + size] = dot_nt(grads[j], wd[CA + at:CA + at + size, :]).astype(BF16)

    loads["wd"].wait()
    make_partial(0)

    pl.semaphore_wait(barrier, len(greet))

    for j in (2, 1, 3):
        device = {"expert": (x + NX - j) % NX}
        copy(grads.at[0], grads.at[j], x_send, x_recv.at[j], device).start()
    for j in (2, 1, 3):
        device = {"expert": (x + NX - j) % NX}
        copy(meta.at[0], meta.at[j], x_send, m_recv.at[j], device).start()

    def send_first(j):
        order = [("y", k) for k in Y_ORDER]
        for place, k in zip((0, 3, 6), Z_ORDER):
            order.insert(place, ("z", k))
        for kind, k in order:
            if kind == "y":
                rows = pl.ds(pl.multiple_of(at_y(k) * RY, RY), RY)
                copy(pa.at[j, rows], ra.at[j, k - 1], s1a_send, s1a_recv.at[j], dp(z, at_y(k))).start()
            else:
                rows = pl.ds(pl.multiple_of(at_z(k) * RZ, RZ), RZ)
                copy(pb.at[j, rows], rb.at[j, k - 1], s1b_send, s1b_recv.at[j], dp(at_z(k), y)).start()

    send_first(0)
    for j in (1, 3, 2):
        await_recv(grads.at[j], x_recv.at[j])
        make_partial(j)
        send_first(j)

    lower = (
        lax.broadcasted_iota(jnp.int32, (TOK, TOK), 0) < lax.broadcasted_iota(jnp.int32, (TOK, TOK), 1)
    ).astype(F32).astype(BF16)
    lane = lax.broadcasted_iota(jnp.int32, (TOK, TOK), 1)

    def make_factors(j):
        group = (x + j) % NX
        me = x.astype(F32)
        rows = meta[j]
        first = rows[2:3] == me
        second = rows[3:4] == me
        weight = jnp.where(first, rows[0:1], 0.0) + jnp.where(second, rows[1:2], 0.0)
        named = jnp.where(first, 1.0, 0.0) + jnp.where(second, 1.0, 0.0)
        named8 = jnp.broadcast_to(named, (8, TOK))
        rank = jnp.dot(named8.astype(BF16), lower, preferred_element_type=F32)[0:1]
        rank = jnp.where(named > 0.0, rank, -1.0)
        row = lax.broadcasted_iota(jnp.int32, (8, TOK), 0)
        columns = jnp.where(row == 0, jnp.broadcast_to(rank, (8, TOK)), jnp.broadcast_to(weight, (8, TOK))).T
        placing = jnp.where(columns[:, 0:1].astype(jnp.int32) == lane, 1.0, 0.0).astype(BF16)
        weight = columns[:, 1:2]
        routed[pl.ds(j * TOK, TOK), :] = (weight * grads[j].astype(F32)).astype(BF16)
        slots = pl.ds(pl.multiple_of(group * TOK, TOK), TOK)
        for at, size in spans(0, HID, 256):
            gate = jnp.dot(placing, sg[slots, at:at + size], preferred_element_type=F32)
            up = jnp.dot(placing, su[slots, at:at + size], preferred_element_type=F32)
            sigmoid = jax.nn.sigmoid(gate)
            swished = gate * sigmoid
            fgate[j, :, at:at + size] = weight * (up * sigmoid * (1.0 + gate * (1.0 - sigmoid)))
            fup[j, :, at:at + size] = weight * swished
            activated[pl.ds(j * TOK, TOK), at:at + size] = (swished * up).astype(BF16)

    my_y = pl.ds(pl.multiple_of(y * RY, RY), RY)
    my_z = pl.ds(pl.multiple_of(z * RZ, RZ), RZ)

    def second(j):
        await_recv(ra.at[j], s1a_recv.at[j])
        total = pa[j, my_y, :].astype(F32)
        for k in range(NY - 1):
            total += ra[j, k].astype(F32)
        sa[j] = total.astype(BF16)

        @pl.when(z != j)
        def _():
            copy(sa.at[j], r2a.at[(j - z + NZ) % NZ - 1], s2a_send, s2a_recv, dp(j, y)).start()

        await_recv(rb.at[j], s1b_recv.at[j])
        total = pb[j, my_z, :].astype(F32)
        for k in range(NZ - 1):
            total += rb[j, k].astype(F32)
        sb[j] = total.astype(BF16)
        for half in range(2):
            owner = 2 * j + half

            @pl.when(y != owner)
            def _():
                copy(
                    sb.at[j, pl.ds(half * 16, 16)], r2b.at[(owner - y + NY) % NY - 1],
                    s2b_send, s2b_recv, dp(z, owner),
                ).start()

    loads["sg"].wait()
    loads["su"].wait()

    def factors(j):
        if j:
            await_recv(meta.at[j], m_recv.at[j])
        make_factors(j)

    factors(0)
    factors(1)
    second(0)
    factors(3)
    second(1)
    factors(2)
    second(3)
    second(2)

    def make_down(at, size):
        gd_out[at:at + size, :] = dot_tn(activated[:, at:at + size], routed[...]).astype(BF16)

    make_down(0, 256)

    await_recv(r2a, s2a_recv)
    total = sa[z].astype(F32)
    for k in range(NZ - 1):
        total += r2a[k].astype(F32)
    acta[z, my_y, :] = total.astype(BF16)
    for k in Z_ORDER:
        copy(acta.at[z, my_y], acta.at[z, my_y], g1a_send, g1a_recv.at[k - 1], dp(at_z(k), y)).start()

    owned = y // 2
    inner = pl.ds(pl.multiple_of((y % 2) * 16, 16), 16)
    owned_rows = pl.ds(pl.multiple_of(z * RZ + (y % 2) * 16, 16), 16)
    await_recv(r2b, s2b_recv)
    total = sb[owned, inner, :].astype(F32)
    for k in range(NY - 1):
        total += r2b[k].astype(F32)
    actb[owned, owned_rows, :] = total.astype(BF16)
    for k in Y_ORDER:
        copy(
            actb.at[owned, owned_rows], actb.at[owned, owned_rows],
            g1b_send, g1b_recv.at[k - 1], dp(z, at_y(k)),
        ).start()

    def gather_y(i):
        j = at_z(i)
        for k in Y_ORDER:
            copy(acta.at[j, my_y], acta.at[j, my_y], g2a_send, g2a_recv.at[i], dp(z, at_y(k))).start()

    def gather_z(i):
        for k in Z_ORDER:
            j = at_z(k + i)
            copy(actb.at[j, my_z], actb.at[j, my_z], g2b_send, g2b_recv.at[i], dp(at_z(k), y)).start()

    gather_y(0)
    make_down(256, 256)
    for k in range(1, NY):
        source = at_y(NY - k)
        rows = pl.ds(pl.multiple_of(z * RZ + (source % 2) * 16, 16), 16)
        await_recv(actb.at[source // 2, rows], g1b_recv.at[k - 1])
    gather_z(0)
    for i in range(1, NZ):
        await_recv(acta.at[at_z(i), my_y], g1a_recv.at[NZ - i - 1])
        gather_y(i)
        gather_z(i)
    make_down(512, 256)

    loads["wg"].wait()
    loads["wu"].wait()

    for i in range(NZ):
        j = at_z(i)
        await_recv(ra.at[i], g2a_recv.at[i])
        await_recv(rb.at[i], g2b_recv.at[i])
        total = jnp.zeros((TOK, FEAT), F32)
        pieces = [(acta, at, at, size) for at, size in spans(0, CA, 256)]
        pieces += [(actb, at, CA + at, size) for at, size in spans(0, CB, 256)]
        for act, at, column, size in pieces:
            value = act[j, :, at:at + size].astype(F32)
            gate = (value * fgate[j, :, column:column + size]).astype(BF16)
            up = (value * fup[j, :, column:column + size]).astype(BF16)
            total += dot_nt(gate, wg[:, column:column + size])
            total += dot_nt(up, wu[:, column:column + size])
        mine[j] = total.astype(BF16)

        @pl.when(j != 0)
        def _():
            copy(mine.at[j], ret.at[j - 1], ret_send, ret_recv, {"expert": (x + j) % NX}).start()

    await_recv(ret, ret_recv)
    total = grads[0].astype(F32)
    returned = mine[0].astype(F32)
    for k in range(NX - 1):
        returned += ret[k].astype(F32)
    ubuf[...] = (total + returned).astype(BF16)
    last = copy(ubuf, vbuf, sec_send, sec_recv, {"section": (s + NS - 1) % NS})
    last.start()

    for j in range(1, NX):
        await_send(grads.at[0], x_send)
        await_send(meta.at[0], x_send)
    for j in range(NX):
        await_send(ra.at[j], s1a_send)
        await_send(rb.at[j], s1b_send)
        await_send(ra.at[j], g2a_send)
        await_send(rb.at[j], g2b_send)
    await_send(r2a, s2a_send)
    await_send(r2a, g1a_send)
    await_send(r2b, g1b_send)
    await_send(r2b, s2b_send)
    await_send(ret, ret_send)

    last.wait_recv()
    up_out[...] = jnp.where(s == NS - 1, jnp.zeros_like(vbuf), vbuf[...])
    last.wait_send()


def on_device(grad_out, routes, route_prob, saved_gate, saved_up, w_gate, w_up, w_down):
    vmem = pltpu.VMEM
    dma = pltpu.SemaphoreType.DMA
    upstream, grad_down = pl.pallas_call(
        kernel,
        out_shape=(
            jax.ShapeDtypeStruct((TOK, FEAT), BF16),
            jax.ShapeDtypeStruct((HID, FEAT), BF16),
        ),
        in_specs=[pl.BlockSpec(memory_space=pltpu.HBM)] * 8,
        out_specs=[pl.BlockSpec(memory_space=vmem)] * 2,
        scratch_shapes=[
            vmem((NX, TOK, FEAT), BF16),
            vmem((NX, 8, TOK), F32),
            vmem((2, TOK), jnp.int32),
            vmem((2, TOK), F32),
            vmem((NX * TOK, HID), BF16),
            vmem((NX * TOK, HID), BF16),
            vmem((FEAT, HID), BF16),
            vmem((FEAT, HID), BF16),
            vmem((HID, FEAT), BF16),
            vmem((NX, TOK, CA), BF16),
            vmem((NX, TOK, CB), BF16),
            vmem((NX, NY - 1, RY, CA), BF16),
            vmem((NX, NZ - 1, RZ, CB), BF16),
            vmem((NX, RY, CA), BF16),
            vmem((NX, RZ, CB), BF16),
            vmem((NZ - 1, RY, CA), BF16),
            vmem((NY - 1, 16, CB), BF16),
            vmem((NX, TOK, CA), BF16),
            vmem((NX, TOK, CB), BF16),
            vmem((NX, TOK, HID), F32),
            vmem((NX, TOK, HID), F32),
            vmem((NX * TOK, HID), BF16),
            vmem((NX * TOK, FEAT), BF16),
            vmem((NX, TOK, FEAT), BF16),
            vmem((NX - 1, TOK, FEAT), BF16),
            vmem((TOK, FEAT), BF16),
            vmem((TOK, FEAT), BF16),
            dma((8,)),
            dma, dma((NX,)), dma((NX,)),
            dma, dma((NX,)), dma, dma((NX,)),
            dma, dma, dma, dma,
            dma, dma((NZ - 1,)), dma, dma((NY - 1,)),
            dma, dma((NZ,)), dma, dma((NZ,)),
            dma, dma, dma, dma,
        ],
        compiler_params=pltpu.CompilerParams(
            collective_id=0, has_side_effects=True, vmem_limit_bytes=48 << 20
        ),
    )(
        grad_out[0], routes[0].T, route_prob[0].T, saved_gate[0, 0], saved_up[0, 0],
        w_gate[0, 0], w_up[0, 0], w_down[0, 0],
    )
    return upstream[None], grad_down[None, None]


def solution(mesh):
    return jax.shard_map(
        on_device,
        mesh=mesh,
        in_specs=(
            P("section", "expert", "dp"),
            P("section", "expert", None),
            P("section", "expert", None),
            P("section", "expert", None, None),
            P("section", "expert", None, None),
            P("section", "expert", "dp", None),
            P("section", "expert", "dp", None),
            P("section", "expert", None, "dp"),
        ),
        out_specs=(P("section", "expert", "dp"), P("section", "expert", None, "dp")),
        check_vma=False,
    )
```

```python
import functools

import jax
import jax.numpy as jnp
from jax import lax
from jax.experimental import pallas as pl
from jax.experimental.pallas import tpu as pltpu
from jax.sharding import PartitionSpec as P

MESH = pl.DeviceIdType.MESH
F32 = jnp.float32
BF16 = jnp.bfloat16

NX, NY, NZ, NS = 4, 8, 4, 6
TOK, FEAT, HID = 128, 128, 768
CA = HID // 2
RY = TOK // NY
Y_ORDER = (4, 3, 5, 2, 6, 1, 7)


def spans(start, stop, step):
    return [(at, min(step, stop - at)) for at in range(start, stop, step)]


def dot_nt(left, right):
    return lax.dot_general(left, right, (((1,), (1,)), ((), ())), preferred_element_type=F32)


def dot_tn(left, right):
    return lax.dot_general(left, right, (((0,), (0,)), ((), ())), preferred_element_type=F32)


def kernel(
    grad_h, routes_h, prob_h, sg_h, su_h, wg_h, wu_h, wd_h,
    up_out, gd_out,
    grads, other, meta, routes, prob, sg, su, wg, wu, wd, wd_half, wg_half, wu_half,
    pa, ra, sa, r2a, acta,
    fgate, fup, activated, routed, mine, ret, ubuf, vbuf,
    load_sem, x_send, x_recv, m_recv, w_send, w_recv, s1a_send, s1a_recv,
    s2a_send, s2a_recv, g2a_send, g2a_recv,
    ret_send, ret_recv, sec_send, sec_recv,
):
    s = lax.axis_index("section")
    x = lax.axis_index("expert")
    d = lax.axis_index("dp")
    y = d % NY
    z = d // NY

    def at_y(k):
        return (y + k) % NY

    half = z % 2
    twin = z + 1 - 2 * half
    far = (z + 2) % NZ
    my_half = pl.ds(pl.multiple_of(half * CA, CA), CA)
    twin_half = pl.ds(pl.multiple_of((1 - half) * CA, CA), CA)

    def dp(zz, yy):
        return {"dp": zz * NY + yy}

    def copy(src, dst, send, recv, device):
        return pltpu.make_async_remote_copy(
            src_ref=src, dst_ref=dst, send_sem=send, recv_sem=recv,
            device_id=device, device_id_type=MESH,
        )

    def await_recv(ref, sem):
        copy(ref, ref, sem, sem, dp(z, y)).wait_recv()

    def await_send(ref, sem):
        copy(ref, ref, sem, sem, dp(z, y)).wait_send()

    sent = []

    loads = {}
    for number, (name, src, dst) in enumerate((
        ("grad", grad_h, grads.at[0]), ("routes", routes_h, routes), ("prob", prob_h, prob),
        ("wd", wd_h, wd), ("sg", sg_h, sg), ("su", su_h, su), ("wg", wg_h, wg), ("wu", wu_h, wu),
    )):
        loads[name] = pltpu.make_async_copy(src, dst, load_sem.at[number])
        loads[name].start()

    barrier = pltpu.get_barrier_semaphore()
    greet = [dp(z, at_y(k)) for k in range(1, NY)] + [dp(far, y)]
    greet += [{"expert": (x + k) % NX} for k in range(1, NX)]
    greet += [{"expert": (x + k) % NX, "dp": twin * NY + y} for k in range(NX)]
    greet += [{"section": (s + 1) % NS}]
    for device in greet:
        pl.semaphore_signal(barrier, inc=1, device_id=device, device_id_type=MESH)

    for name in ("grad", "routes", "prob"):
        loads[name].wait()
    meta[0, 0:2, :] = prob[...]
    meta[0, 2:4, :] = routes[...].astype(F32)
    meta[0, 4:8, :] = jnp.zeros((4, TOK), F32)

    def own_partial(j):
        return dot_nt(grads[j], wd[my_half, :])

    def make_partial(j, own):
        pa[j] = (own + dot_nt(other[j], wd_half[...])).astype(BF16)

    loads["wd"].wait()
    own = own_partial(0)

    pl.semaphore_wait(barrier, len(greet))

    def to_twin(src, dst, send, recv, j):
        copy(src, dst, send, recv, {"expert": (x + NX - j) % NX, "dp": twin * NY + y}).start()

    to_twin(grads.at[0], other.at[0], x_send, x_recv.at[1, 0], 0)
    to_twin(wd.at[twin_half], wd_half, w_send, w_recv.at[0], 0)
    for j in (2, 1, 3):
        to_twin(grads.at[0], other.at[j], x_send, x_recv.at[1, j], j)
        device = {"expert": (x + NX - j) % NX}
        copy(grads.at[0], grads.at[j], x_send, x_recv.at[0, j], device).start()
    for j in (2, 1, 3):
        device = {"expert": (x + NX - j) % NX}
        copy(meta.at[0], meta.at[j], x_send, m_recv.at[j], device).start()
    sent.extend([(grads, x_send), (grads.at[pl.ds(0, 3)], x_send)] + [(meta.at[0], x_send)] * 3)

    def tiles(count):
        return pa.at[0, pl.ds(0, 16 * count)]

    def rows_y(k):
        return pl.ds(pl.multiple_of(at_y(k) * RY, RY), RY)

    def to_y(src, dst, send, recv, k):
        copy(src, dst, send, recv, dp(z, at_y(k))).start()

    def send_first(j):
        for k in Y_ORDER:
            to_y(pa.at[j, rows_y(k)], ra.at[j, k - 1], s1a_send, s1a_recv.at[j], k)
        sent.append((tiles(7), s1a_send))

    await_recv(wd_half, w_recv.at[0])
    await_recv(other.at[0], x_recv.at[1, 0])
    make_partial(0, own)
    send_first(0)
    for j in (1, 3, 2):
        await_recv(grads.at[j], x_recv.at[0, j])
        own = own_partial(j)
        await_recv(other.at[j], x_recv.at[1, j])
        make_partial(j, own)
        send_first(j)

    loads["wg"].wait()
    loads["wu"].wait()
    to_twin(wg.at[:, twin_half], wg_half, w_send, w_recv.at[1], 0)
    to_twin(wu.at[:, twin_half], wu_half, w_send, w_recv.at[2], 0)
    sent.extend([(wd_half, w_send), (wg_half, w_send), (wu_half, w_send)])

    lower = (
        lax.broadcasted_iota(jnp.int32, (TOK, TOK), 0) < lax.broadcasted_iota(jnp.int32, (TOK, TOK), 1)
    ).astype(F32).astype(BF16)
    lane = lax.broadcasted_iota(jnp.int32, (TOK, TOK), 1)

    def make_factors(j):
        group = (x + j) % NX
        me = x.astype(F32)
        rows = meta[j]
        first = rows[2:3] == me
        second = rows[3:4] == me
        weight = jnp.where(first, rows[0:1], 0.0) + jnp.where(second, rows[1:2], 0.0)
        named = jnp.where(first, 1.0, 0.0) + jnp.where(second, 1.0, 0.0)
        named8 = jnp.broadcast_to(named, (8, TOK))
        rank = jnp.dot(named8.astype(BF16), lower, preferred_element_type=F32)[0:1]
        rank = jnp.where(named > 0.0, rank, -1.0)
        row = lax.broadcasted_iota(jnp.int32, (8, TOK), 0)
        columns = jnp.where(row == 0, jnp.broadcast_to(rank, (8, TOK)), jnp.broadcast_to(weight, (8, TOK))).T
        placing = jnp.where(columns[:, 0:1].astype(jnp.int32) == lane, 1.0, 0.0).astype(BF16)
        weight = columns[:, 1:2]
        routed[pl.ds(j * TOK, TOK), :] = (weight * grads[j].astype(F32)).astype(BF16)
        slots = pl.ds(pl.multiple_of(group * TOK, TOK), TOK)
        for side, columns in ((0, my_half), (1, twin_half)):
            gate = jnp.dot(placing, sg[slots, columns], preferred_element_type=F32)
            up = jnp.dot(placing, su[slots, columns], preferred_element_type=F32)
            sigmoid = jax.nn.sigmoid(gate)
            swished = gate * sigmoid
            if side == 0:
                fgate[j] = weight * (up * sigmoid * (1.0 + gate * (1.0 - sigmoid)))
                fup[j] = weight * swished
            activated[pl.ds(j * TOK, TOK), columns] = (swished * up).astype(BF16)

    my_y = pl.ds(pl.multiple_of(y * RY, RY), RY)

    def second(j):
        await_recv(tiles(7), s1a_recv.at[j])
        total = pa[j, my_y, :].astype(F32)
        for k in range(NY - 1):
            total += ra[j, k].astype(F32)
        sa[j] = total.astype(BF16)
        copy(sa.at[j], r2a.at[j], s2a_send, s2a_recv.at[j], dp(far, y)).start()
        sent.append((tiles(1), s2a_send))

    loads["sg"].wait()
    loads["su"].wait()

    def factors(j):
        if j:
            await_recv(meta.at[j], m_recv.at[j])
        make_factors(j)

    factors(0)
    second(0)
    factors(1)
    second(1)
    factors(3)
    second(3)
    factors(2)
    second(2)

    def make_down(at, size):
        gd_out[at:at + size, :] = dot_tn(activated[:, at:at + size], routed[...]).astype(BF16)

    def third(j):
        await_recv(r2a.at[j], s2a_recv.at[j])
        total = sa[j].astype(F32) + r2a[j].astype(F32)
        acta[j, my_y, :] = total.astype(BF16)
        mine_a = acta.at[j, my_y]
        for k in Y_ORDER:
            to_y(mine_a, mine_a, g2a_send, g2a_recv.at[j], k)
        sent.append((tiles(7), g2a_send))

    third(0)
    third(1)
    third(3)
    third(2)
    make_down(0, 256)
    make_down(256, 256)
    make_down(512, 256)

    await_recv(wg_half, w_recv.at[1])
    await_recv(wu_half, w_recv.at[2])

    for j in (1, 3, 2, 0):
        await_recv(tiles(7), g2a_recv.at[j])
        value = acta[j].astype(F32)
        gate = (value * fgate[j]).astype(BF16)
        up = (value * fup[j]).astype(BF16)
        device = {"expert": (x + j) % NX, "dp": twin * NY + y}
        mine[1, j] = (dot_nt(gate, wg_half[...]) + dot_nt(up, wu_half[...])).astype(BF16)
        copy(mine.at[1, j], ret.at[1, j], ret_send, ret_recv.at[1, j], device).start()
        mine[0, j] = (dot_nt(gate, wg[:, my_half]) + dot_nt(up, wu[:, my_half])).astype(BF16)
        if j:
            device = {"expert": (x + j) % NX}
            copy(mine.at[0, j], ret.at[0, j], ret_send, ret_recv.at[0, j], device).start()

    sent.extend([(grads, ret_send), (grads.at[pl.ds(0, 3)], ret_send)])
    for j in (1, 3, 2, 0):
        await_recv(ret.at[1, j], ret_recv.at[1, j])
        if j:
            await_recv(ret.at[0, j], ret_recv.at[0, j])
    total = grads[0].astype(F32)
    returned = mine[0, 0].astype(F32) + ret[1, 0].astype(F32)
    for j in range(1, NX):
        returned += ret[0, j].astype(F32) + ret[1, j].astype(F32)
    ubuf[...] = (total + returned).astype(BF16)
    last = copy(ubuf, vbuf, sec_send, sec_recv, {"section": (s + NS - 1) % NS})
    last.start()

    for ref, sem in sent:
        await_send(ref, sem)
    last.wait_recv()
    up_out[...] = jnp.where(s == NS - 1, jnp.zeros_like(vbuf), vbuf[...])
    last.wait_send()


def on_device(grad_out, routes, route_prob, saved_gate, saved_up, w_gate, w_up, w_down):
    vmem = pltpu.VMEM
    dma = pltpu.SemaphoreType.DMA
    upstream, grad_down = pl.pallas_call(
        kernel,
        out_shape=(
            jax.ShapeDtypeStruct((TOK, FEAT), BF16),
            jax.ShapeDtypeStruct((HID, FEAT), BF16),
        ),
        in_specs=[pl.BlockSpec(memory_space=pltpu.HBM)] * 8,
        out_specs=[pl.BlockSpec(memory_space=vmem)] * 2,
        scratch_shapes=[
            vmem((NX, TOK, FEAT), BF16),
            vmem((NX, TOK, FEAT), BF16),
            vmem((NX, 8, TOK), F32),
            vmem((2, TOK), jnp.int32),
            vmem((2, TOK), F32),
            vmem((NX * TOK, HID), BF16),
            vmem((NX * TOK, HID), BF16),
            vmem((FEAT, HID), BF16),
            vmem((FEAT, HID), BF16),
            vmem((HID, FEAT), BF16),
            vmem((CA, FEAT), BF16),
            vmem((FEAT, CA), BF16),
            vmem((FEAT, CA), BF16),
            vmem((NX, TOK, CA), BF16),
            vmem((NX, NY - 1, RY, CA), BF16),
            vmem((NX, RY, CA), BF16),
            vmem((NX, RY, CA), BF16),
            vmem((NX, TOK, CA), BF16),
            vmem((NX, TOK, CA), F32),
            vmem((NX, TOK, CA), F32),
            vmem((NX * TOK, HID), BF16),
            vmem((NX * TOK, FEAT), BF16),
            vmem((2, NX, TOK, FEAT), BF16),
            vmem((2, NX, TOK, FEAT), BF16),
            vmem((TOK, FEAT), BF16),
            vmem((TOK, FEAT), BF16),
            dma((8,)),
            dma, dma((2, NX)), dma((NX,)),
            dma, dma((3,)), dma, dma((NX,)),
            dma, dma((NX,)), dma, dma((NX,)),
            dma, dma((2, NX)), dma, dma,
        ],
        compiler_params=pltpu.CompilerParams(
            collective_id=0, has_side_effects=True, vmem_limit_bytes=48 << 20
        ),
    )(*(
        pltpu.with_memory_space_constraint(value, pltpu.HBM)
        for value in (
            grad_out[0], routes[0].T, route_prob[0].T, saved_gate[0, 0], saved_up[0, 0],
            w_gate[0, 0], w_up[0, 0], w_down[0, 0],
        )
    ))
    return upstream[None], grad_down[None, None]


def solution(mesh):
    return jax.shard_map(
        on_device,
        mesh=mesh,
        in_specs=(
            P("section", "expert", "dp"),
            P("section", "expert", None),
            P("section", "expert", None),
            P("section", "expert", None, None),
            P("section", "expert", None, None),
            P("section", "expert", "dp", None),
            P("section", "expert", "dp", None),
            P("section", "expert", None, "dp"),
        ),
        out_specs=(P("section", "expert", "dp"), P("section", "expert", None, "dp")),
        check_vma=False,
    )
```

```python
import functools

import jax
import jax.numpy as jnp
from jax import lax
from jax.experimental import pallas as pl
from jax.experimental.pallas import tpu as pltpu
from jax.sharding import PartitionSpec as P

MESH = pl.DeviceIdType.MESH
F32 = jnp.float32
BF16 = jnp.bfloat16

NX, NY, NZ, NS = 4, 8, 4, 6
TOK, FEAT, HID = 128, 128, 768
CA = HID // 2
RY = TOK // NY
Y_ORDER = (4, 3, 5, 2, 6, 1, 7)


def spans(start, stop, step):
    return [(at, min(step, stop - at)) for at in range(start, stop, step)]


def dot_nt(left, right):
    return lax.dot_general(left, right, (((1,), (1,)), ((), ())), preferred_element_type=F32)


def dot_tn(left, right):
    return lax.dot_general(left, right, (((0,), (0,)), ((), ())), preferred_element_type=F32)


def kernel(
    grad_h, routes_h, prob_h, sg_h, su_h, wg_h, wu_h, wd_h,
    up_out, gd_out,
    grads, other, meta, routes, prob, sg, su, wg, wu, wd, wd_half, wg_half, wu_half,
    pa, ra, sa, r2a, acta,
    fgate, fup, activated, routed, mine, ret, ubuf, vbuf,
    load_sem, x_send, x_recv, m_recv, w_send, w_recv, s1a_send, s1a_recv,
    s2a_send, s2a_recv, g2a_send, g2a_recv,
    ret_send, ret_recv, sec_send, sec_recv, turn,
):
    s = lax.axis_index("section")
    x = lax.axis_index("expert")
    d = lax.axis_index("dp")
    y = d % NY
    z = d // NY

    def at_y(k):
        return (y + k) % NY

    half = z % 2
    twin = z + 1 - 2 * half
    far = (z + 2) % NZ
    my_half = pl.ds(pl.multiple_of(half * CA, CA), CA)
    twin_half = pl.ds(pl.multiple_of((1 - half) * CA, CA), CA)

    def dp(zz, yy):
        return {"dp": zz * NY + yy}

    def copy(src, dst, send, recv, device):
        return pltpu.make_async_remote_copy(
            src_ref=src, dst_ref=dst, send_sem=send, recv_sem=recv,
            device_id=device, device_id_type=MESH,
        )

    def await_recv(ref, sem):
        copy(ref, ref, sem, sem, dp(z, y)).wait_recv()

    def await_send(ref, sem):
        copy(ref, ref, sem, sem, dp(z, y)).wait_send()

    live = s != 0
    first_half = jnp.logical_and(live, s % 2 == 0)
    second_half = s % 2 == 1
    loads = {}
    for number, (name, src, dst) in enumerate((
        ("grad", grad_h, grads.at[0]), ("routes", routes_h, routes), ("prob", prob_h, prob),
        ("wd", wd_h, wd), ("sg", sg_h, sg), ("su", su_h, su), ("wg", wg_h, wg), ("wu", wu_h, wu),
    )):
        loads[name] = pltpu.make_async_copy(src, dst, load_sem.at[number])
        loads[name].start()

    barrier = pltpu.get_barrier_semaphore()
    greet = [dp(z, at_y(k)) for k in range(1, NY)] + [dp(far, y)]
    greet += [{"expert": (x + k) % NX} for k in range(1, NX)]
    greet += [{"expert": (x + k) % NX, "dp": twin * NY + y} for k in range(NX)]
    for device in greet:
        pl.semaphore_signal(barrier, inc=1, device_id=device, device_id_type=MESH)
    expected = len(greet) + jnp.where(s > 0, 1, 0)

    @pl.when(s < NS - 1)
    def _():
        device = {"section": (s + 1) % NS}
        pl.semaphore_signal(barrier, inc=1, device_id=device, device_id_type=MESH)

    expected += jnp.where(s % 2 == 0, 1, 0)

    @pl.when(s % 2 == 1)
    def _():
        device = {"section": (s + NS - 1) % NS}
        pl.semaphore_signal(barrier, inc=1, device_id=device, device_id_type=MESH)

    for name in ("grad", "routes", "prob"):
        loads[name].wait()
    meta[0, 0:2, :] = prob[...]
    meta[0, 2:4, :] = routes[...].astype(F32)
    meta[0, 4:8, :] = jnp.zeros((4, TOK), F32)

    def own_partial(j):
        return dot_nt(grads[j], wd[my_half, :])

    def make_partial(j, own):
        pa[j] = (own + dot_nt(other[j], wd_half[...])).astype(BF16)

    loads["wd"].wait()
    own = own_partial(0)

    pl.semaphore_wait(barrier, expected)

    def pass_turn():
        pl.semaphore_signal(turn, inc=1, device_id={"section": (s + 1) % NS}, device_id_type=MESH)

    @pl.when(s == 0)
    def _():
        pass_turn()

    def to_twin(src, dst, send, recv, j):
        copy(src, dst, send, recv, {"expert": (x + NX - j) % NX, "dp": twin * NY + y}).start()

    to_twin(grads.at[0], other.at[0], x_send, x_recv.at[1, 0], 0)
    to_twin(wd.at[twin_half], wd_half, w_send, w_recv.at[0], 0)
    for j in (2, 1, 3):
        to_twin(grads.at[0], other.at[j], x_send, x_recv.at[1, j], j)
        device = {"expert": (x + NX - j) % NX}
        copy(grads.at[0], grads.at[j], x_send, x_recv.at[0, j], device).start()
    for j in (2, 1, 3):
        device = {"expert": (x + NX - j) % NX}
        copy(meta.at[0], meta.at[j], x_send, m_recv.at[j], device).start()

    def tiles(count):
        return pa.at[0, pl.ds(0, 16 * count)]

    def rows_y(k):
        return pl.ds(pl.multiple_of(at_y(k) * RY, RY), RY)

    def to_y(src, dst, send, recv, k):
        copy(src, dst, send, recv, dp(z, at_y(k))).start()

    def send_first(j):
        for k in Y_ORDER:
            to_y(pa.at[j, rows_y(k)], ra.at[j, k - 1], s1a_send, s1a_recv.at[j], k)

    lower = (
        lax.broadcasted_iota(jnp.int32, (TOK, TOK), 0) < lax.broadcasted_iota(jnp.int32, (TOK, TOK), 1)
    ).astype(F32).astype(BF16)
    lane = lax.broadcasted_iota(jnp.int32, (TOK, TOK), 1)

    def make_factors(j):
        group = (x + j) % NX
        me = x.astype(F32)
        rows = meta[j]
        first = rows[2:3] == me
        second = rows[3:4] == me
        weight = jnp.where(first, rows[0:1], 0.0) + jnp.where(second, rows[1:2], 0.0)
        named = jnp.where(first, 1.0, 0.0) + jnp.where(second, 1.0, 0.0)
        named8 = jnp.broadcast_to(named, (8, TOK))
        rank = jnp.dot(named8.astype(BF16), lower, preferred_element_type=F32)[0:1]
        rank = jnp.where(named > 0.0, rank, -1.0)
        row = lax.broadcasted_iota(jnp.int32, (8, TOK), 0)
        columns = jnp.where(row == 0, jnp.broadcast_to(rank, (8, TOK)), jnp.broadcast_to(weight, (8, TOK))).T
        placing = jnp.where(columns[:, 0:1].astype(jnp.int32) == lane, 1.0, 0.0).astype(BF16)
        weight = columns[:, 1:2]
        routed[pl.ds(j * TOK, TOK), :] = (weight * grads[j].astype(F32)).astype(BF16)
        slots = pl.ds(pl.multiple_of(group * TOK, TOK), TOK)
        for side, columns in ((0, my_half), (1, twin_half)):
            gate = jnp.dot(placing, sg[slots, columns], preferred_element_type=F32)
            up = jnp.dot(placing, su[slots, columns], preferred_element_type=F32)
            sigmoid = jax.nn.sigmoid(gate)
            swished = gate * sigmoid
            if side == 0:
                fgate[j] = weight * (up * sigmoid * (1.0 + gate * (1.0 - sigmoid)))
                fup[j] = weight * swished
            activated[pl.ds(j * TOK, TOK), columns] = (swished * up).astype(BF16)

    def factors(j):
        if j:
            await_recv(meta.at[j], m_recv.at[j])
        make_factors(j)

    await_recv(wd_half, w_recv.at[0])
    await_recv(other.at[0], x_recv.at[1, 0])
    make_partial(0, own)

    @pl.when(first_half)
    def _():
        send_first(0)

    loads["sg"].wait()
    loads["su"].wait()
    factors(0)
    for j in (1, 3, 2):
        await_recv(grads.at[j], x_recv.at[0, j])
        own = own_partial(j)
        await_recv(other.at[j], x_recv.at[1, j])
        make_partial(j, own)

        @pl.when(first_half)
        def _():
            send_first(j)

    loads["wg"].wait()
    loads["wu"].wait()

    @pl.when(live)
    def _():
        to_twin(wg.at[:, twin_half], wg_half, w_send, w_recv.at[1], 0)
        to_twin(wu.at[:, twin_half], wu_half, w_send, w_recv.at[2], 0)

    my_y = pl.ds(pl.multiple_of(y * RY, RY), RY)

    def second(j):
        await_recv(tiles(7), s1a_recv.at[j])
        total = pa[j, my_y, :].astype(F32)
        for k in range(NY - 1):
            total += ra[j, k].astype(F32)
        sa[j] = total.astype(BF16)
        copy(sa.at[j], r2a.at[j], s2a_send, s2a_recv.at[j], dp(far, y)).start()

    factors(1)
    factors(3)
    factors(2)

    def make_down(at, size):
        gd_out[at:at + size, :] = dot_tn(activated[:, at:at + size], routed[...]).astype(BF16)

    def third(j):
        await_recv(r2a.at[j], s2a_recv.at[j])
        total = sa[j].astype(F32) + r2a[j].astype(F32)
        acta[j, my_y, :] = total.astype(BF16)
        mine_a = acta.at[j, my_y]
        for k in Y_ORDER:
            to_y(mine_a, mine_a, g2a_send, g2a_recv.at[j], k)

    def reduce_rest():
        second(3)
        second(2)
        for j in (1, 3, 2, 0):
            third(j)

    @pl.when(first_half)
    def _():
        second(0)
        second(1)
        for j in range(NX):
            await_send(tiles(7), s1a_send)
        pass_turn()
        reduce_rest()

    @pl.when(second_half)
    def _():
        pl.semaphore_wait(turn, 1)
        for j in (0, 1, 3, 2):
            send_first(j)
        second(0)
        second(1)
        reduce_rest()
        for j in range(NX):
            await_send(tiles(7), s1a_send)


    last = copy(ubuf, vbuf, sec_send, sec_recv, {"section": (s + NS - 1) % NS})

    @pl.when(live)
    def _():
        await_recv(wg_half, w_recv.at[1])
        await_recv(wu_half, w_recv.at[2])
        for j in (1, 3, 2, 0):
            await_recv(tiles(7), g2a_recv.at[j])
            value = acta[j].astype(F32)
            gate = (value * fgate[j]).astype(BF16)
            up = (value * fup[j]).astype(BF16)
            device = {"expert": (x + j) % NX, "dp": twin * NY + y}
            mine[1, j] = (dot_nt(gate, wg_half[...]) + dot_nt(up, wu_half[...])).astype(BF16)
            copy(mine.at[1, j], ret.at[1, j], ret_send, ret_recv.at[1, j], device).start()
            mine[0, j] = (dot_nt(gate, wg[:, my_half]) + dot_nt(up, wu[:, my_half])).astype(BF16)
            if j:
                device = {"expert": (x + j) % NX}
                copy(mine.at[0, j], ret.at[0, j], ret_send, ret_recv.at[0, j], device).start()

        make_down(0, 256)
        for j in (1, 3, 2, 0):
            await_recv(ret.at[1, j], ret_recv.at[1, j])
            if j:
                await_recv(ret.at[0, j], ret_recv.at[0, j])
        total = grads[0].astype(F32)
        returned = mine[0, 0].astype(F32) + ret[1, 0].astype(F32)
        for j in range(1, NX):
            returned += ret[0, j].astype(F32) + ret[1, j].astype(F32)
        ubuf[...] = (total + returned).astype(BF16)
        last.start()
        make_down(256, 256)
        make_down(512, 256)
        for ref, sem in (
            [(wg_half, w_send), (wu_half, w_send), (grads, ret_send), (grads.at[pl.ds(0, 3)], ret_send)]
            + [(tiles(4), s2a_send)] + [(tiles(7), g2a_send)] * NX
        ):
            await_send(ref, sem)
        last.wait_send()

    @pl.when(s == 0)
    def _():
        for at in (0, 256, 512):
            make_down(at, 256)

    await_send(wd_half, w_send)
    await_send(grads, x_send)
    await_send(grads.at[pl.ds(0, 3)], x_send)
    for j in range(1, NX):
        await_send(meta.at[0], x_send)

    @pl.when(s == NS - 1)
    def _():
        up_out[...] = jnp.zeros_like(up_out)

    @pl.when(s != NS - 1)
    def _():
        last.wait_recv()
        up_out[...] = vbuf[...]


def on_device(grad_out, routes, route_prob, saved_gate, saved_up, w_gate, w_up, w_down):
    vmem = pltpu.VMEM
    dma = pltpu.SemaphoreType.DMA
    upstream, grad_down = pl.pallas_call(
        kernel,
        out_shape=(
            jax.ShapeDtypeStruct((TOK, FEAT), BF16),
            jax.ShapeDtypeStruct((HID, FEAT), BF16),
        ),
        in_specs=[pl.BlockSpec(memory_space=pltpu.HBM)] * 8,
        out_specs=[pl.BlockSpec(memory_space=vmem)] * 2,
        scratch_shapes=[
            vmem((NX, TOK, FEAT), BF16),
            vmem((NX, TOK, FEAT), BF16),
            vmem((NX, 8, TOK), F32),
            vmem((2, TOK), jnp.int32),
            vmem((2, TOK), F32),
            vmem((NX * TOK, HID), BF16),
            vmem((NX * TOK, HID), BF16),
            vmem((FEAT, HID), BF16),
            vmem((FEAT, HID), BF16),
            vmem((HID, FEAT), BF16),
            vmem((CA, FEAT), BF16),
            vmem((FEAT, CA), BF16),
            vmem((FEAT, CA), BF16),
            vmem((NX, TOK, CA), BF16),
            vmem((NX, NY - 1, RY, CA), BF16),
            vmem((NX, RY, CA), BF16),
            vmem((NX, RY, CA), BF16),
            vmem((NX, TOK, CA), BF16),
            vmem((NX, TOK, CA), F32),
            vmem((NX, TOK, CA), F32),
            vmem((NX * TOK, HID), BF16),
            vmem((NX * TOK, FEAT), BF16),
            vmem((2, NX, TOK, FEAT), BF16),
            vmem((2, NX, TOK, FEAT), BF16),
            vmem((TOK, FEAT), BF16),
            vmem((TOK, FEAT), BF16),
            dma((8,)),
            dma, dma((2, NX)), dma((NX,)),
            dma, dma((3,)), dma, dma((NX,)),
            dma, dma((NX,)), dma, dma((NX,)),
            dma, dma((2, NX)), dma, dma,
            pltpu.SemaphoreType.REGULAR,
        ],
        compiler_params=pltpu.CompilerParams(
            collective_id=0, has_side_effects=True, vmem_limit_bytes=48 << 20
        ),
    )(*(
        pltpu.with_memory_space_constraint(value, pltpu.HBM)
        for value in (
            grad_out[0], routes[0].T, route_prob[0].T, saved_gate[0, 0], saved_up[0, 0],
            w_gate[0, 0], w_up[0, 0], w_down[0, 0],
        )
    ))
    return upstream[None], grad_down[None, None]


def solution(mesh):
    return jax.shard_map(
        on_device,
        mesh=mesh,
        in_specs=(
            P("section", "expert", "dp"),
            P("section", "expert", None),
            P("section", "expert", None),
            P("section", "expert", None, None),
            P("section", "expert", None, None),
            P("section", "expert", "dp", None),
            P("section", "expert", "dp", None),
            P("section", "expert", None, "dp"),
        ),
        out_specs=(P("section", "expert", "dp"), P("section", "expert", None, "dp")),
        check_vma=False,
    )
```

```python
import functools

import jax
import jax.numpy as jnp
from jax import lax
from jax.experimental import pallas as pl
from jax.experimental.pallas import tpu as pltpu
from jax.sharding import PartitionSpec as P

MESH = pl.DeviceIdType.MESH
F32 = jnp.float32
BF16 = jnp.bfloat16

NX, NY, NZ, NS = 4, 8, 4, 6
TOK, FEAT, HID = 128, 128, 768
CA = HID // 2
RY = TOK // NY
Y_ORDER = (4, 3, 5, 2, 6, 1, 7)


def spans(start, stop, step):
    return [(at, min(step, stop - at)) for at in range(start, stop, step)]


def dot_nt(left, right):
    return lax.dot_general(left, right, (((1,), (1,)), ((), ())), preferred_element_type=F32)


def dot_tn(left, right):
    return lax.dot_general(left, right, (((0,), (0,)), ((), ())), preferred_element_type=F32)


def kernel(
    grad_h, routes_h, prob_h, sg_h, su_h, wg_h, wu_h, wd_h,
    up_out, gd_out,
    grads, other, meta, routes, prob, sg, su, wg, wu, wd, wd_half, wide, both,
    pa, ra, sa, r2a, acta,
    fgate, fup, activated, routed, mine, ret, ubuf, vbuf,
    load_sem, x_send, x_recv, m_recv, w_send, w_recv, s1a_send, s1a_recv,
    s2a_send, s2a_recv, g2a_send, g2a_recv,
    ret_send, ret_recv, sec_send, sec_recv, turn,
):
    s = lax.axis_index("section")
    x = lax.axis_index("expert")
    d = lax.axis_index("dp")
    y = d % NY
    z = d // NY

    def at_y(k):
        return (y + k) % NY

    half = z % 2
    twin = z + 1 - 2 * half
    far = (z + 2) % NZ
    my_half = pl.ds(pl.multiple_of(half * CA, CA), CA)
    twin_half = pl.ds(pl.multiple_of((1 - half) * CA, CA), CA)

    def dp(zz, yy):
        return {"dp": zz * NY + yy}

    def copy(src, dst, send, recv, device):
        return pltpu.make_async_remote_copy(
            src_ref=src, dst_ref=dst, send_sem=send, recv_sem=recv,
            device_id=device, device_id_type=MESH,
        )

    def await_recv(ref, sem):
        copy(ref, ref, sem, sem, dp(z, y)).wait_recv()

    def await_send(ref, sem):
        copy(ref, ref, sem, sem, dp(z, y)).wait_send()

    live = s != 0
    first_half = jnp.logical_and(live, s % 2 == 0)
    second_half = s % 2 == 1
    loads = {}
    for number, (name, src, dst) in enumerate((
        ("grad", grad_h, grads.at[0]), ("routes", routes_h, routes), ("prob", prob_h, prob),
        ("wd", wd_h, wd), ("sg", sg_h, sg), ("su", su_h, su), ("wg", wg_h, wg), ("wu", wu_h, wu),
    )):
        loads[name] = pltpu.make_async_copy(src, dst, load_sem.at[number])
        loads[name].start()

    barrier = pltpu.get_barrier_semaphore()
    greet = [dp(z, at_y(k)) for k in range(1, NY)] + [dp(far, y)]
    greet += [{"expert": (x + k) % NX} for k in range(1, NX)]
    greet += [{"expert": (x + k) % NX, "dp": twin * NY + y} for k in range(NX)]
    for device in greet:
        pl.semaphore_signal(barrier, inc=1, device_id=device, device_id_type=MESH)
    expected = len(greet) + jnp.where(s > 0, 1, 0)

    @pl.when(s < NS - 1)
    def _():
        device = {"section": (s + 1) % NS}
        pl.semaphore_signal(barrier, inc=1, device_id=device, device_id_type=MESH)

    expected += jnp.where(s % 2 == 0, 1, 0)

    @pl.when(s % 2 == 1)
    def _():
        device = {"section": (s + NS - 1) % NS}
        pl.semaphore_signal(barrier, inc=1, device_id=device, device_id_type=MESH)

    for name in ("grad", "routes", "prob"):
        loads[name].wait()
    meta[0, 0:2, :] = prob[...]
    meta[0, 2:4, :] = routes[...].astype(F32)
    meta[0, 4:8, :] = jnp.zeros((4, TOK), F32)

    def own_partial(j):
        return dot_nt(grads[j], wd[my_half, :])

    def make_partial(j, own):
        pa[j] = (own + dot_nt(other[j], wd_half[...])).astype(BF16)

    loads["wd"].wait()
    own = own_partial(0)

    pl.semaphore_wait(barrier, expected)

    def pass_turn():
        pl.semaphore_signal(turn, inc=1, device_id={"section": (s + 1) % NS}, device_id_type=MESH)

    @pl.when(s == 0)
    def _():
        pass_turn()

    def to_twin(src, dst, send, recv, j):
        copy(src, dst, send, recv, {"expert": (x + NX - j) % NX, "dp": twin * NY + y}).start()

    to_twin(grads.at[0], other.at[0], x_send, x_recv.at[1, 0], 0)
    to_twin(wd.at[twin_half], wd_half, w_send, w_recv.at[0], 0)
    for j in (2, 1, 3):
        to_twin(grads.at[0], other.at[j], x_send, x_recv.at[1, j], j)
        device = {"expert": (x + NX - j) % NX}
        copy(grads.at[0], grads.at[j], x_send, x_recv.at[0, j], device).start()
    for j in (2, 1, 3):
        device = {"expert": (x + NX - j) % NX}
        copy(meta.at[0], meta.at[j], x_send, m_recv.at[j], device).start()

    def tiles(count):
        return pa.at[0, pl.ds(0, 16 * count)]

    def rows_y(k):
        return pl.ds(pl.multiple_of(at_y(k) * RY, RY), RY)

    def to_y(src, dst, send, recv, k):
        copy(src, dst, send, recv, dp(z, at_y(k))).start()

    def send_first(j):
        for k in Y_ORDER:
            to_y(pa.at[j, rows_y(k)], ra.at[j, k - 1], s1a_send, s1a_recv.at[j], k)

    lower = (
        lax.broadcasted_iota(jnp.int32, (TOK, TOK), 0) < lax.broadcasted_iota(jnp.int32, (TOK, TOK), 1)
    ).astype(F32).astype(BF16)
    lane = lax.broadcasted_iota(jnp.int32, (TOK, TOK), 1)

    def make_factors(j):
        group = (x + j) % NX
        me = x.astype(F32)
        rows = meta[j]
        first = rows[2:3] == me
        second = rows[3:4] == me
        weight = jnp.where(first, rows[0:1], 0.0) + jnp.where(second, rows[1:2], 0.0)
        named = jnp.where(first, 1.0, 0.0) + jnp.where(second, 1.0, 0.0)
        named8 = jnp.broadcast_to(named, (8, TOK))
        rank = jnp.dot(named8.astype(BF16), lower, preferred_element_type=F32)[0:1]
        rank = jnp.where(named > 0.0, rank, -1.0)
        row = lax.broadcasted_iota(jnp.int32, (8, TOK), 0)
        columns = jnp.where(row == 0, jnp.broadcast_to(rank, (8, TOK)), jnp.broadcast_to(weight, (8, TOK))).T
        placing = jnp.where(columns[:, 0:1].astype(jnp.int32) == lane, 1.0, 0.0).astype(BF16)
        weight = columns[:, 1:2]
        routed[pl.ds(j * TOK, TOK), :] = (weight * grads[j].astype(F32)).astype(BF16)
        slots = pl.ds(pl.multiple_of(group * TOK, TOK), TOK)
        for side, columns in ((0, my_half), (1, twin_half)):
            gate = jnp.dot(placing, sg[slots, columns], preferred_element_type=F32)
            up = jnp.dot(placing, su[slots, columns], preferred_element_type=F32)
            sigmoid = jax.nn.sigmoid(gate)
            swished = gate * sigmoid
            if side == 0:
                fgate[j] = weight * (up * sigmoid * (1.0 + gate * (1.0 - sigmoid)))
                fup[j] = weight * swished
            activated[pl.ds(j * TOK, TOK), columns] = (swished * up).astype(BF16)

    def factors(j):
        if j:
            await_recv(meta.at[j], m_recv.at[j])
        make_factors(j)

    await_recv(wd_half, w_recv.at[0])
    await_recv(other.at[0], x_recv.at[1, 0])
    make_partial(0, own)

    @pl.when(first_half)
    def _():
        send_first(0)

    loads["sg"].wait()
    loads["su"].wait()
    factors(0)
    for j in (1, 3, 2):
        await_recv(grads.at[j], x_recv.at[0, j])
        own = own_partial(j)
        await_recv(other.at[j], x_recv.at[1, j])
        make_partial(j, own)

        @pl.when(first_half)
        def _():
            send_first(j)

    loads["wg"].wait()
    loads["wu"].wait()

    @pl.when(live)
    def _():
        to_twin(wg.at[:, twin_half], wide.at[pl.ds(FEAT, FEAT), pl.ds(0, CA)], w_send, w_recv.at[1], 0)
        to_twin(wu.at[:, twin_half], wide.at[pl.ds(FEAT, FEAT), pl.ds(CA, CA)], w_send, w_recv.at[2], 0)
        wide[0:FEAT, 0:CA] = wg[:, my_half]
        wide[0:FEAT, CA:HID] = wu[:, my_half]

    my_y = pl.ds(pl.multiple_of(y * RY, RY), RY)

    def second(j):
        await_recv(tiles(7), s1a_recv.at[j])
        total = pa[j, my_y, :].astype(F32)
        for k in range(NY - 1):
            total += ra[j, k].astype(F32)
        sa[j] = total.astype(BF16)
        copy(sa.at[j], r2a.at[j], s2a_send, s2a_recv.at[j], dp(far, y)).start()

    factors(1)
    factors(3)
    factors(2)

    def make_down(at, size):
        gd_out[at:at + size, :] = dot_tn(activated[:, at:at + size], routed[...]).astype(BF16)

    def third(j):
        await_recv(r2a.at[j], s2a_recv.at[j])
        total = sa[j].astype(F32) + r2a[j].astype(F32)
        acta[j, my_y, :] = total.astype(BF16)
        mine_a = acta.at[j, my_y]
        for k in Y_ORDER:
            to_y(mine_a, mine_a, g2a_send, g2a_recv.at[j], k)

    def reduce_rest():
        second(3)
        second(2)
        for j in (1, 3, 2, 0):
            third(j)

    @pl.when(first_half)
    def _():
        second(0)
        second(1)
        for j in range(NX):
            await_send(tiles(7), s1a_send)
        pass_turn()
        reduce_rest()

    @pl.when(second_half)
    def _():
        pl.semaphore_wait(turn, 1)
        for j in (0, 1, 3, 2):
            send_first(j)
        second(0)
        second(1)
        reduce_rest()
        for j in range(NX):
            await_send(tiles(7), s1a_send)


    lasts = [
        copy(
            ubuf.at[pl.ds(at, 32)], vbuf.at[pl.ds(at, 32)], sec_send, sec_recv.at[at // 32],
            {"section": (s + NS - 1) % NS},
        )
        for at in range(0, TOK, 32)
    ]

    @pl.when(live)
    def _():
        await_recv(wide.at[pl.ds(FEAT, FEAT), pl.ds(0, CA)], w_recv.at[1])
        await_recv(wide.at[pl.ds(FEAT, FEAT), pl.ds(CA, CA)], w_recv.at[2])
        for j in (1, 3, 2, 0):
            await_recv(tiles(7), g2a_recv.at[j])
            value = acta[j].astype(F32)
            both[j, :, 0:CA] = (value * fgate[j]).astype(BF16)
            both[j, :, CA:HID] = (value * fup[j]).astype(BF16)
            slot_grads = dot_nt(both[j], wide[...])
            device = {"expert": (x + j) % NX, "dp": twin * NY + y}
            mine[1, j] = slot_grads[:, FEAT:].astype(BF16)
            copy(mine.at[1, j], ret.at[1, j], ret_send, ret_recv.at[1, j], device).start()
            mine[0, j] = slot_grads[:, :FEAT].astype(BF16)
            if j:
                device = {"expert": (x + j) % NX}
                copy(mine.at[0, j], ret.at[0, j], ret_send, ret_recv.at[0, j], device).start()

        make_down(0, 256)
        for j in (1, 3, 2, 0):
            await_recv(ret.at[1, j], ret_recv.at[1, j])
            if j:
                await_recv(ret.at[0, j], ret_recv.at[0, j])
        for part, last in enumerate(lasts):
            rows = pl.ds(part * 32, 32)
            total = grads[0, rows].astype(F32)
            returned = mine[0, 0, rows].astype(F32) + ret[1, 0, rows].astype(F32)
            for j in range(1, NX):
                returned += ret[0, j, rows].astype(F32) + ret[1, j, rows].astype(F32)
            ubuf[rows, :] = (total + returned).astype(BF16)
            last.start()
        make_down(256, 256)
        make_down(512, 256)
        for ref, sem in (
            [(wd_half, w_send), (wd_half, w_send), (grads, ret_send), (grads.at[pl.ds(0, 3)], ret_send)]
            + [(tiles(4), s2a_send)] + [(tiles(7), g2a_send)] * NX
        ):
            await_send(ref, sem)
        await_send(ubuf, sec_send)

    @pl.when(s == 0)
    def _():
        for at in (0, 256, 512):
            make_down(at, 256)

    await_send(wd_half, w_send)
    await_send(grads, x_send)
    await_send(grads.at[pl.ds(0, 3)], x_send)
    for j in range(1, NX):
        await_send(meta.at[0], x_send)

    @pl.when(s == NS - 1)
    def _():
        up_out[...] = jnp.zeros_like(up_out)

    @pl.when(s != NS - 1)
    def _():
        for last in lasts:
            last.wait_recv()
        up_out[...] = vbuf[...]


def on_device(grad_out, routes, route_prob, saved_gate, saved_up, w_gate, w_up, w_down):
    vmem = pltpu.VMEM
    dma = pltpu.SemaphoreType.DMA
    upstream, grad_down = pl.pallas_call(
        kernel,
        out_shape=(
            jax.ShapeDtypeStruct((TOK, FEAT), BF16),
            jax.ShapeDtypeStruct((HID, FEAT), BF16),
        ),
        in_specs=[pl.BlockSpec(memory_space=pltpu.HBM)] * 8,
        out_specs=[pl.BlockSpec(memory_space=vmem)] * 2,
        scratch_shapes=[
            vmem((NX, TOK, FEAT), BF16),
            vmem((NX, TOK, FEAT), BF16),
            vmem((NX, 8, TOK), F32),
            vmem((2, TOK), jnp.int32),
            vmem((2, TOK), F32),
            vmem((NX * TOK, HID), BF16),
            vmem((NX * TOK, HID), BF16),
            vmem((FEAT, HID), BF16),
            vmem((FEAT, HID), BF16),
            vmem((HID, FEAT), BF16),
            vmem((CA, FEAT), BF16),
            vmem((2 * FEAT, HID), BF16),
            vmem((NX, TOK, HID), BF16),
            vmem((NX, TOK, CA), BF16),
            vmem((NX, NY - 1, RY, CA), BF16),
            vmem((NX, RY, CA), BF16),
            vmem((NX, RY, CA), BF16),
            vmem((NX, TOK, CA), BF16),
            vmem((NX, TOK, CA), F32),
            vmem((NX, TOK, CA), F32),
            vmem((NX * TOK, HID), BF16),
            vmem((NX * TOK, FEAT), BF16),
            vmem((2, NX, TOK, FEAT), BF16),
            vmem((2, NX, TOK, FEAT), BF16),
            vmem((TOK, FEAT), BF16),
            vmem((TOK, FEAT), BF16),
            dma((8,)),
            dma, dma((2, NX)), dma((NX,)),
            dma, dma((3,)), dma, dma((NX,)),
            dma, dma((NX,)), dma, dma((NX,)),
            dma, dma((2, NX)), dma, dma((4,)),
            pltpu.SemaphoreType.REGULAR,
        ],
        compiler_params=pltpu.CompilerParams(
            collective_id=0, has_side_effects=True, vmem_limit_bytes=48 << 20
        ),
    )(*(
        pltpu.with_memory_space_constraint(value, pltpu.HBM)
        for value in (
            grad_out[0], routes[0].T, route_prob[0].T, saved_gate[0, 0], saved_up[0, 0],
            w_gate[0, 0], w_up[0, 0], w_down[0, 0],
        )
    ))
    return upstream[None], grad_down[None, None]


def solution(mesh):
    return jax.shard_map(
        on_device,
        mesh=mesh,
        in_specs=(
            P("section", "expert", "dp"),
            P("section", "expert", None),
            P("section", "expert", None),
            P("section", "expert", None, None),
            P("section", "expert", None, None),
            P("section", "expert", "dp", None),
            P("section", "expert", "dp", None),
            P("section", "expert", None, "dp"),
        ),
        out_specs=(P("section", "expert", "dp"), P("section", "expert", None, "dp")),
        check_vma=False,
    )
```

```python
import functools

import jax
import jax.numpy as jnp
from jax import lax
from jax.experimental import pallas as pl
from jax.experimental.pallas import tpu as pltpu
from jax.sharding import PartitionSpec as P

MESH = pl.DeviceIdType.MESH
F32 = jnp.float32
BF16 = jnp.bfloat16

NX, NY, NZ, NS = 4, 8, 4, 6
TOK, FEAT, HID = 128, 128, 768
CA = HID // 2
RY = TOK // NY
Y_ORDER = (4, 3, 5, 2, 6, 1, 7)


def spans(start, stop, step):
    return [(at, min(step, stop - at)) for at in range(start, stop, step)]


def dot_nt(left, right):
    return lax.dot_general(left, right, (((1,), (1,)), ((), ())), preferred_element_type=F32)


def dot_tn(left, right):
    return lax.dot_general(left, right, (((0,), (0,)), ((), ())), preferred_element_type=F32)


def kernel(
    grad_h, routes_h, prob_h, sg_h, su_h, wg_h, wu_h, wd_h,
    up_out, gd_out,
    grads, other, meta, routes, prob, sg, su, wg, wu, wd, wd_half, wide, both,
    pa, ra, sa, r2a, acta,
    fgate, fup, activated, routed, mine, ret, ubuf, vbuf,
    load_sem, x_send, x_recv, m_recv, w_send, w_recv, s1a_send, s1a_recv,
    s2a_send, s2a_recv, g2a_send, g2a_recv,
    ret_send, ret_recv, sec_send, sec_recv, turn,
):
    s = lax.axis_index("section")
    x = lax.axis_index("expert")
    d = lax.axis_index("dp")
    y = d % NY
    z = d // NY

    def at_y(k):
        return (y + k) % NY

    half = z % 2
    twin = z + 1 - 2 * half
    far = (z + 2) % NZ
    my_half = pl.ds(pl.multiple_of(half * CA, CA), CA)
    twin_half = pl.ds(pl.multiple_of((1 - half) * CA, CA), CA)

    def dp(zz, yy):
        return {"dp": zz * NY + yy}

    def copy(src, dst, send, recv, device):
        return pltpu.make_async_remote_copy(
            src_ref=src, dst_ref=dst, send_sem=send, recv_sem=recv,
            device_id=device, device_id_type=MESH,
        )

    def await_recv(ref, sem):
        copy(ref, ref, sem, sem, dp(z, y)).wait_recv()

    def await_send(ref, sem):
        copy(ref, ref, sem, sem, dp(z, y)).wait_send()

    live = s != 0
    first_half = jnp.logical_and(live, s % 2 == 0)
    second_half = s % 2 == 1
    loads = {}
    for number, (name, src, dst) in enumerate((
        ("grad", grad_h, grads.at[0]), ("routes", routes_h, routes), ("prob", prob_h, prob),
        ("wd", wd_h, wd), ("sg", sg_h, sg), ("su", su_h, su), ("wg", wg_h, wg), ("wu", wu_h, wu),
    )):
        loads[name] = pltpu.make_async_copy(src, dst, load_sem.at[number])
        loads[name].start()

    barrier = pltpu.get_barrier_semaphore()
    greet = [dp(z, at_y(k)) for k in Y_ORDER] + [dp(far, y)]
    greet += [{"expert": (x + k) % NX} for k in range(1, NX)]
    greet += [{"expert": (x + k) % NX, "dp": twin * NY + y} for k in range(NX)]
    for device in greet:
        pl.semaphore_signal(barrier, inc=1, device_id=device, device_id_type=MESH)
    expected = len(greet) + jnp.where(s > 0, 1, 0)

    @pl.when(s < NS - 1)
    def _():
        device = {"section": (s + 1) % NS}
        pl.semaphore_signal(barrier, inc=1, device_id=device, device_id_type=MESH)

    expected += jnp.where(s % 2 == 0, 1, 0)

    @pl.when(s % 2 == 1)
    def _():
        device = {"section": (s + NS - 1) % NS}
        pl.semaphore_signal(barrier, inc=1, device_id=device, device_id_type=MESH)

    for name in ("grad", "routes", "prob"):
        loads[name].wait()
    meta[0, 0:2, :] = prob[...]
    meta[0, 2:4, :] = routes[...].astype(F32)
    meta[0, 4:8, :] = jnp.zeros((4, TOK), F32)

    def own_partial(j):
        return dot_nt(grads[j], wd[my_half, :])

    def make_partial(j, own):
        pa[j] = (own + dot_nt(other[j], wd_half[...])).astype(BF16)

    loads["wd"].wait()
    own = own_partial(0)

    pl.semaphore_wait(barrier, expected)

    def pass_turn():
        pl.semaphore_signal(turn, inc=1, device_id={"section": (s + 1) % NS}, device_id_type=MESH)

    @pl.when(s == 0)
    def _():
        pass_turn()

    def to_twin(src, dst, send, recv, j):
        copy(src, dst, send, recv, {"expert": (x + NX - j) % NX, "dp": twin * NY + y}).start()

    to_twin(grads.at[0], other.at[0], x_send, x_recv.at[1, 0], 0)
    to_twin(wd.at[twin_half], wd_half, w_send, w_recv.at[0], 0)
    for j in (2, 1, 3):
        to_twin(grads.at[0], other.at[j], x_send, x_recv.at[1, j], j)
        device = {"expert": (x + NX - j) % NX}
        copy(grads.at[0], grads.at[j], x_send, x_recv.at[0, j], device).start()
    for j in (2, 1, 3):
        device = {"expert": (x + NX - j) % NX}
        copy(meta.at[0], meta.at[j], x_send, m_recv.at[j], device).start()

    def tiles(count):
        return pa.at[0, pl.ds(0, 16 * count)]

    def rows_y(k):
        return pl.ds(pl.multiple_of(at_y(k) * RY, RY), RY)

    def to_y(src, dst, send, recv, k):
        copy(src, dst, send, recv, dp(z, at_y(k))).start()

    def send_first(j):
        for k in Y_ORDER:
            to_y(pa.at[j, rows_y(k)], ra.at[j, k - 1], s1a_send, s1a_recv.at[j], k)

    lower = (
        lax.broadcasted_iota(jnp.int32, (TOK, TOK), 0) < lax.broadcasted_iota(jnp.int32, (TOK, TOK), 1)
    ).astype(F32).astype(BF16)
    lane = lax.broadcasted_iota(jnp.int32, (TOK, TOK), 1)

    def make_factors(j):
        group = (x + j) % NX
        me = x.astype(F32)
        rows = meta[j]
        first = rows[2:3] == me
        second = rows[3:4] == me
        weight = jnp.where(first, rows[0:1], 0.0) + jnp.where(second, rows[1:2], 0.0)
        named = jnp.where(first, 1.0, 0.0) + jnp.where(second, 1.0, 0.0)
        named8 = jnp.broadcast_to(named, (8, TOK))
        rank = jnp.dot(named8.astype(BF16), lower, preferred_element_type=F32)[0:1]
        rank = jnp.where(named > 0.0, rank, -1.0)
        row = lax.broadcasted_iota(jnp.int32, (8, TOK), 0)
        columns = jnp.where(row == 0, jnp.broadcast_to(rank, (8, TOK)), jnp.broadcast_to(weight, (8, TOK))).T
        placing = jnp.where(columns[:, 0:1].astype(jnp.int32) == lane, 1.0, 0.0).astype(BF16)
        weight = columns[:, 1:2]
        routed[pl.ds(j * TOK, TOK), :] = (weight * grads[j].astype(F32)).astype(BF16)
        slots = pl.ds(pl.multiple_of(group * TOK, TOK), TOK)
        for side, columns in ((0, my_half), (1, twin_half)):
            gate = jnp.dot(placing, sg[slots, columns], preferred_element_type=F32)
            up = jnp.dot(placing, su[slots, columns], preferred_element_type=F32)
            sigmoid = jax.nn.sigmoid(gate)
            swished = gate * sigmoid
            if side == 0:
                fgate[j] = weight * (up * sigmoid * (1.0 + gate * (1.0 - sigmoid)))
                fup[j] = weight * swished
            activated[pl.ds(j * TOK, TOK), columns] = (swished * up).astype(BF16)

    def factors(j):
        if j:
            await_recv(meta.at[j], m_recv.at[j])
        make_factors(j)

    await_recv(wd_half, w_recv.at[0])
    await_recv(other.at[0], x_recv.at[1, 0])
    make_partial(0, own)

    @pl.when(first_half)
    def _():
        send_first(0)

    loads["sg"].wait()
    loads["su"].wait()
    factors(0)
    for j in (1, 3, 2):
        await_recv(grads.at[j], x_recv.at[0, j])
        own = own_partial(j)
        await_recv(other.at[j], x_recv.at[1, j])
        make_partial(j, own)

        @pl.when(first_half)
        def _():
            send_first(j)

    loads["wg"].wait()
    loads["wu"].wait()

    @pl.when(live)
    def _():
        to_twin(wg.at[:, twin_half], wide.at[pl.ds(FEAT, FEAT), pl.ds(0, CA)], w_send, w_recv.at[1], 0)
        to_twin(wu.at[:, twin_half], wide.at[pl.ds(FEAT, FEAT), pl.ds(CA, CA)], w_send, w_recv.at[2], 0)
        wide[0:FEAT, 0:CA] = wg[:, my_half]
        wide[0:FEAT, CA:HID] = wu[:, my_half]

    my_y = pl.ds(pl.multiple_of(y * RY, RY), RY)

    def second(j):
        await_recv(tiles(7), s1a_recv.at[j])
        total = pa[j, my_y, :].astype(F32)
        for k in range(NY - 1):
            total += ra[j, k].astype(F32)
        sa[j] = total.astype(BF16)
        copy(sa.at[j], r2a.at[j], s2a_send, s2a_recv.at[j], dp(far, y)).start()

    factors(1)
    factors(3)
    factors(2)

    def make_down(at, size):
        gd_out[at:at + size, :] = dot_tn(activated[:, at:at + size], routed[...]).astype(BF16)

    def third(j):
        await_recv(r2a.at[j], s2a_recv.at[j])
        total = sa[j].astype(F32) + r2a[j].astype(F32)
        acta[j, my_y, :] = total.astype(BF16)
        mine_a = acta.at[j, my_y]
        for k in Y_ORDER:
            to_y(mine_a, mine_a, g2a_send, g2a_recv.at[j], k)

    def reduce_rest():
        second(3)
        second(2)
        for j in (1, 3, 2, 0):
            third(j)

    @pl.when(first_half)
    def _():
        second(0)
        second(1)
        pass_turn()
        reduce_rest()
        for j in range(NX):
            await_send(tiles(7), s1a_send)

    @pl.when(second_half)
    def _():
        pl.semaphore_wait(turn, 1)
        for j in (0, 1, 3, 2):
            send_first(j)
        second(0)
        second(1)
        reduce_rest()
        for j in range(NX):
            await_send(tiles(7), s1a_send)


    lasts = [
        copy(
            ubuf.at[pl.ds(at, 32)], vbuf.at[pl.ds(at, 32)], sec_send, sec_recv.at[at // 32],
            {"section": (s + NS - 1) % NS},
        )
        for at in range(0, TOK, 32)
    ]

    @pl.when(live)
    def _():
        await_recv(wide.at[pl.ds(FEAT, FEAT), pl.ds(0, CA)], w_recv.at[1])
        await_recv(wide.at[pl.ds(FEAT, FEAT), pl.ds(CA, CA)], w_recv.at[2])
        for j in (1, 3, 2, 0):
            await_recv(tiles(7), g2a_recv.at[j])
            value = acta[j].astype(F32)
            both[j, :, 0:CA] = (value * fgate[j]).astype(BF16)
            both[j, :, CA:HID] = (value * fup[j]).astype(BF16)
            slot_grads = dot_nt(both[j], wide[...])
            device = {"expert": (x + j) % NX, "dp": twin * NY + y}
            mine[1, j] = slot_grads[:, FEAT:].astype(BF16)
            copy(mine.at[1, j], ret.at[1, j], ret_send, ret_recv.at[1, j], device).start()
            mine[0, j] = slot_grads[:, :FEAT].astype(BF16)
            if j:
                device = {"expert": (x + j) % NX}
                copy(mine.at[0, j], ret.at[0, j], ret_send, ret_recv.at[0, j], device).start()

        make_down(0, 256)
        for j in (1, 3, 2, 0):
            await_recv(ret.at[1, j], ret_recv.at[1, j])
            if j:
                await_recv(ret.at[0, j], ret_recv.at[0, j])
        for part, last in enumerate(lasts):
            rows = pl.ds(part * 32, 32)
            total = grads[0, rows].astype(F32)
            returned = mine[0, 0, rows].astype(F32) + ret[1, 0, rows].astype(F32)
            for j in range(1, NX):
                returned += ret[0, j, rows].astype(F32) + ret[1, j, rows].astype(F32)
            ubuf[rows, :] = (total + returned).astype(BF16)
            last.start()
        make_down(256, 256)
        make_down(512, 256)
        for ref, sem in (
            [(wd_half, w_send), (wd_half, w_send), (grads, ret_send), (grads.at[pl.ds(0, 3)], ret_send)]
            + [(tiles(4), s2a_send)] + [(tiles(7), g2a_send)] * NX
        ):
            await_send(ref, sem)
        await_send(ubuf, sec_send)

    @pl.when(s == 0)
    def _():
        for at in (0, 256, 512):
            make_down(at, 256)

    await_send(wd_half, w_send)
    await_send(grads, x_send)
    await_send(grads.at[pl.ds(0, 3)], x_send)
    for j in range(1, NX):
        await_send(meta.at[0], x_send)

    @pl.when(s == NS - 1)
    def _():
        up_out[...] = jnp.zeros_like(up_out)

    @pl.when(s != NS - 1)
    def _():
        for last in lasts:
            last.wait_recv()
        up_out[...] = vbuf[...]


def on_device(grad_out, routes, route_prob, saved_gate, saved_up, w_gate, w_up, w_down):
    vmem = pltpu.VMEM
    dma = pltpu.SemaphoreType.DMA
    upstream, grad_down = pl.pallas_call(
        kernel,
        out_shape=(
            jax.ShapeDtypeStruct((TOK, FEAT), BF16),
            jax.ShapeDtypeStruct((HID, FEAT), BF16),
        ),
        in_specs=[pl.BlockSpec(memory_space=pltpu.HBM)] * 8,
        out_specs=[pl.BlockSpec(memory_space=vmem)] * 2,
        scratch_shapes=[
            vmem((NX, TOK, FEAT), BF16),
            vmem((NX, TOK, FEAT), BF16),
            vmem((NX, 8, TOK), F32),
            vmem((2, TOK), jnp.int32),
            vmem((2, TOK), F32),
            vmem((NX * TOK, HID), BF16),
            vmem((NX * TOK, HID), BF16),
            vmem((FEAT, HID), BF16),
            vmem((FEAT, HID), BF16),
            vmem((HID, FEAT), BF16),
            vmem((CA, FEAT), BF16),
            vmem((2 * FEAT, HID), BF16),
            vmem((NX, TOK, HID), BF16),
            vmem((NX, TOK, CA), BF16),
            vmem((NX, NY - 1, RY, CA), BF16),
            vmem((NX, RY, CA), BF16),
            vmem((NX, RY, CA), BF16),
            vmem((NX, TOK, CA), BF16),
            vmem((NX, TOK, CA), F32),
            vmem((NX, TOK, CA), F32),
            vmem((NX * TOK, HID), BF16),
            vmem((NX * TOK, FEAT), BF16),
            vmem((2, NX, TOK, FEAT), BF16),
            vmem((2, NX, TOK, FEAT), BF16),
            vmem((TOK, FEAT), BF16),
            vmem((TOK, FEAT), BF16),
            dma((8,)),
            dma, dma((2, NX)), dma((NX,)),
            dma, dma((3,)), dma, dma((NX,)),
            dma, dma((NX,)), dma, dma((NX,)),
            dma, dma((2, NX)), dma, dma((4,)),
            pltpu.SemaphoreType.REGULAR,
        ],
        compiler_params=pltpu.CompilerParams(
            collective_id=0, has_side_effects=True, vmem_limit_bytes=48 << 20
        ),
    )(*(
        pltpu.with_memory_space_constraint(value, pltpu.HBM)
        for value in (
            grad_out[0], routes[0].T, route_prob[0].T, saved_gate[0, 0], saved_up[0, 0],
            w_gate[0, 0], w_up[0, 0], w_down[0, 0],
        )
    ))
    return upstream[None], grad_down[None, None]


def solution(mesh):
    return jax.shard_map(
        on_device,
        mesh=mesh,
        in_specs=(
            P("section", "expert", "dp"),
            P("section", "expert", None),
            P("section", "expert", None),
            P("section", "expert", None, None),
            P("section", "expert", None, None),
            P("section", "expert", "dp", None),
            P("section", "expert", "dp", None),
            P("section", "expert", None, "dp"),
        ),
        out_specs=(P("section", "expert", "dp"), P("section", "expert", None, "dp")),
        check_vma=False,
    )
```
